32 devices in a mesh: gx: 4 (over z), gy: 4 (over y, x), gz: 2 (over core).
Axes of the slice: x: 2, y: 2, z: 4, core: 2. Of those that a mesh axis runs over, the one named last changes fastest.
Arguments:
- species_partial_mass: float32 [9, 16, 128, 512], P(None, 'gz', 'gx', 'gy'), may hold values from 0.2 to 2
- motion_components: float32 [2, 16, 128, 512], P(None, 'gz', 'gx', 'gy'), may hold values from -6 to 6
- grid_stretch_main: float32 [2, 16, 128, 512], P(None, 'gz', 'gx', 'gy'), may hold values from 0.5 to 1.5
- grid_stretch_cross: float32 [2, 16, 128, 512], P(None, 'gz', 'gx', 'gy'), may hold values from -1.2 to 1.2
- volume_scaling_reciprocal: float32 [16, 128, 512], P('gz', 'gx', 'gy'), may hold values from 0.5 to 2
- kelvin_field: float32 [16, 128, 512], P('gz', 'gx', 'gy'), may hold values from 900 to 2500
- first_dir_piece_solver: float32 [32, 32], replicated, may hold values from -1 to 1
- first_dir_rhs_condense: float32 [4, 32], replicated, may hold values from -1 to 1
- first_dir_border_spread: float32 [32, 4], replicated, may hold values from -3 to 3
- first_dir_small_solver: float32 [16, 16], P('gx'), may hold values from -1 to 2
- second_dir_piece_solver: float32 [128, 128], replicated, may hold values from -0.5 to 0.5
- second_dir_rhs_condense: float32 [4, 128], replicated, may hold values from -0.5 to 0.5
- second_dir_border_spread: float32 [128, 4], replicated, may hold values from -3 to 3
- second_dir_small_solver: float32 [16, 16], P('gy'), may hold values from -2 to 3
- speed_factor_ln_reference: float32 [19], replicated, may hold values from -1 to 1
- kelvin_exponent_each: float32 [19], replicated, may hold values from -1 to 1
- arrhenius_energy_kelvin: float32 [19], replicated, may hold values from 0 to 6000
- consumed_species_flags: int32 [19, 9], replicated, may hold values 0 or 1
- stoich_net_shift: int32 [19, 9], replicated, may hold values from -2 to 2
- boundary_supplying_volume: int32 [4, 4, 512], P('gx', 'gy', 'gz'), may hold values from 0 to 32767
- boundary_target_volume: int32 [4, 4, 512], P('gx', 'gy', 'gz'), may hold values from 0 to 32767
- boundary_slot_used: int32 [4, 4, 512], P('gx', 'gy', 'gz'), may hold values 0 or 1
- boundary_transfer_weight: float32 [4, 4, 512], P('gx', 'gy', 'gz'), may hold values from 0.2 to 2
- open_volume_flags: int32 [16, 128, 512], P('gz', 'gx', 'gy'), may hold values 0 or 1
Outputs:
- section_rhs: float32 [9, 16, 128, 512], P(None, 'gz', 'gx', 'gy')
- section_state: float32 [9, 16, 128, 512], P(None, 'gz', 'gx', 'gy')
The draws below stay inside these ranges and needn't reach their ends.
All inputs are finite; a program needn't handle non-finite values. No bound on the sum of `boundary_slot_used` or of `open_volume_flags` on one device may be relied on, other than what follows from the above.
Results may differ from the reference program's by a relative error of at most 0.000068.
Values sent between devices are 32-bit elements; how exact they have to be, the bound alone decides.
A program may use at most 128 MiB of HBM per device.

```python
import math
import jax
import jax.numpy as jnp
from jax import lax

NS = 9
REACTION_TOTAL = 19
K = 4
CX = 32
CY = 128
CZ = 8
FMAX = 256
CELLS = 32768
VOLUMES_ALONG_E = 128
VOLUMES_ALONG_N = 512
VOLUMES_ALONG_U = 16
KX = 16
KY = 16
N_GX = 4
N_GY = 4
N_GZ = 2


def dense_system(key, order, spread):
    noise = jnp.clip(jax.random.normal(key, (order, order), jnp.float32), -4.0, 4.0)
    return jnp.eye(order, dtype=jnp.float32) + noise * (spread / order ** 0.5)


def draw_first_dir_small_solver(key, part):
    key = jax.random.fold_in(key, 11)
    return dense_system(key, KX, 1.0)


def draw_second_dir_small_solver(key, part):
    key = jax.random.fold_in(key, 23)
    return dense_system(key, KY, 1.0)


def set_ends(values, own_key, least, top_value):
    longest = values.shape.index(max(values.shape))
    spots = []
    for shift in (0, 1):
        where = [jax.random.randint(jax.random.fold_in(own_key, axis), (), 0, length) for axis, length in enumerate(values.shape)]
        where[longest] = (where[longest] + shift) % values.shape[longest]
        spots.append(tuple(where))
    return values.at[spots[0]].set(least).at[spots[1]].set(top_value)


def shard_levels(rng, dims, cuts, low, largest):
    loudness = 1.0
    for position, parts in cuts:
        steps = jax.random.uniform(jax.random.fold_in(jax.random.fold_in(rng, 6), position), (parts,), jnp.float32, low / len(cuts), largest / len(cuts))
        loudness = loudness * jnp.repeat(jnp.exp(steps), dims[position] // parts).reshape((-1,) + (1,) * (len(dims) - 1 - position))
    return loudness


def gaussian(rng, shape, width, reach, pieces=(), kind=jnp.bfloat16):
    loudness = shard_levels(rng, shape, pieces, -0.22, 0.18) if pieces else 1.0
    drawn = jax.random.normal(rng, shape, jnp.float32) * width * loudness
    return jnp.minimum(jnp.maximum(drawn, -reach), reach).astype(kind)


def setup_inputs(seed: int = 0) -> dict:
    key_list = jax.random.split(jax.random.key(seed), 25)
    return {
        "species_partial_mass": jnp.clip(jnp.exp(math.log(2.0) - 2.3025851 * jax.random.uniform(key_list[0], (NS, VOLUMES_ALONG_U, VOLUMES_ALONG_E, VOLUMES_ALONG_N), jnp.float32) ** shard_levels(key_list[0], (NS, VOLUMES_ALONG_U, VOLUMES_ALONG_E, VOLUMES_ALONG_N), ((1, 2), (2, 4), (3, 4)), -0.2, 0.2)), 0.2, 2.0),
        "motion_components": gaussian(key_list[1], (2, VOLUMES_ALONG_U, VOLUMES_ALONG_E, VOLUMES_ALONG_N), 1.0, 6.0, ((1, 2), (2, 4), (3, 4)), jnp.float32),
        "grid_stretch_main": jnp.clip(0.5 + 1.0 * jax.random.uniform(key_list[2], (2, VOLUMES_ALONG_U, VOLUMES_ALONG_E, VOLUMES_ALONG_N), jnp.float32) ** shard_levels(key_list[2], (2, VOLUMES_ALONG_U, VOLUMES_ALONG_E, VOLUMES_ALONG_N), ((1, 2), (2, 4), (3, 4)), -0.2, 0.2), 0.5, 1.5),
        "grid_stretch_cross": gaussian(key_list[3], (2, VOLUMES_ALONG_U, VOLUMES_ALONG_E, VOLUMES_ALONG_N), 0.3, 1.2, ((1, 2), (2, 4), (3, 4)), jnp.float32),
        "volume_scaling_reciprocal": jnp.clip(jnp.exp(math.log(2.0) - 1.3862944 * jax.random.uniform(key_list[4], (VOLUMES_ALONG_U, VOLUMES_ALONG_E, VOLUMES_ALONG_N), jnp.float32) ** shard_levels(key_list[4], (VOLUMES_ALONG_U, VOLUMES_ALONG_E, VOLUMES_ALONG_N), ((0, 2), (1, 4), (2, 4)), -0.2, 0.2)), 0.5, 2.0),
        "kelvin_field": jnp.clip(900.0 + 1600.0 * jax.random.uniform(key_list[5], (VOLUMES_ALONG_U, VOLUMES_ALONG_E, VOLUMES_ALONG_N), jnp.float32) ** shard_levels(key_list[5], (VOLUMES_ALONG_U, VOLUMES_ALONG_E, VOLUMES_ALONG_N), ((0, 2), (1, 4), (2, 4)), -0.2, 0.2), 900.0, 2500.0),
        "first_dir_piece_solver": gaussian(key_list[6], (CX, CX), CX ** -0.5, 1.0, (), jnp.float32),
        "first_dir_rhs_condense": gaussian(key_list[7], (K, CX), CX ** -0.5, 1.0, (), jnp.float32),
        "first_dir_border_spread": gaussian(key_list[8], (CX, K), K ** -0.5, 3.0, (), jnp.float32),
        "first_dir_small_solver": draw_first_dir_small_solver(jax.random.fold_in(key_list[24], 71), 0),
        "second_dir_piece_solver": gaussian(key_list[10], (CY, CY), CY ** -0.5, 0.5, (), jnp.float32),
        "second_dir_rhs_condense": gaussian(key_list[11], (K, CY), CY ** -0.5, 0.5, (), jnp.float32),
        "second_dir_border_spread": gaussian(key_list[12], (CY, K), K ** -0.5, 3.0, (), jnp.float32),
        "second_dir_small_solver": draw_second_dir_small_solver(jax.random.fold_in(key_list[24], 71), 0),
        "speed_factor_ln_reference": jnp.clip(jax.random.uniform(key_list[14], (REACTION_TOTAL,), jnp.float32, -1.0, 1.0), -1.0, 1.0),
        "kelvin_exponent_each": jnp.clip(jax.random.uniform(key_list[15], (REACTION_TOTAL,), jnp.float32, -1.0, 1.0), -1.0, 1.0),
        "arrhenius_energy_kelvin": jnp.clip(jax.random.uniform(key_list[16], (REACTION_TOTAL,), jnp.float32, 0.0, 6000.0), 0.0, 6000.0),
        "consumed_species_flags": set_ends((jax.random.randint(key_list[17], (REACTION_TOTAL, NS), 0, 4) < 1).astype(jnp.int32), jax.random.fold_in(key_list[17], 1), 0, 1),
        "stoich_net_shift": set_ends(jax.random.randint(key_list[18], (REACTION_TOTAL, NS), -2, 3), jax.random.fold_in(key_list[18], 1), -2, 2).astype(jnp.int32),
        "boundary_supplying_volume": set_ends(jax.random.randint(key_list[19], (N_GX, N_GY, N_GZ * FMAX), 0, CELLS), jax.random.fold_in(key_list[19], 1), 0, CELLS - 1).astype(jnp.int32),
        "boundary_target_volume": set_ends(jax.random.randint(key_list[20], (N_GX, N_GY, N_GZ * FMAX), 0, CELLS), jax.random.fold_in(key_list[20], 1), 0, CELLS - 1).astype(jnp.int32),
        "boundary_slot_used": set_ends((jax.random.randint(key_list[21], (N_GX, N_GY, N_GZ * FMAX), 0, 4) < 3).astype(jnp.int32), jax.random.fold_in(key_list[21], 1), 0, 1),
        "boundary_transfer_weight": jnp.clip(jnp.exp(math.log(2.0) - 2.3025851 * jax.random.uniform(key_list[22], (N_GX, N_GY, N_GZ * FMAX), jnp.float32) ** shard_levels(key_list[22], (N_GX, N_GY, N_GZ * FMAX), ((0, 4), (1, 4), (2, 2)), -0.2, 0.2)), 0.2, 2.0),
        "open_volume_flags": set_ends((jax.random.randint(key_list[23], (VOLUMES_ALONG_U, VOLUMES_ALONG_E, VOLUMES_ALONG_N), 0, 8) < 7).astype(jnp.int32), jax.random.fold_in(key_list[23], 1), 0, 1),
    }


HI = lax.Precision.HIGHEST


def to_blocks(field):
    field = field.reshape(NS, N_GZ, CZ, N_GX, CX, N_GY, CY)
    return field.transpose(3, 5, 1, 0, 2, 4, 6).reshape(N_GX * N_GY * N_GZ, NS, CZ * CX * CY)


def from_blocks(field):
    field = field.reshape(N_GX, N_GY, N_GZ, NS, CZ, CX, CY)
    return field.transpose(3, 2, 4, 0, 5, 1, 6).reshape(NS, VOLUMES_ALONG_U, VOLUMES_ALONG_E, VOLUMES_ALONG_N)


def wall_block(source_cells, target_cells, outgoing, incoming):
    total = jnp.zeros((NS, CZ * CX * CY), jnp.float32)
    total = total.at[:, target_cells].add(incoming)
    return total.at[:, source_cells].add(-outgoing)


def reference(species_partial_mass, motion_components, grid_stretch_main, grid_stretch_cross, volume_scaling_reciprocal, kelvin_field, first_dir_piece_solver, first_dir_rhs_condense, first_dir_border_spread, first_dir_small_solver, second_dir_piece_solver, second_dir_rhs_condense, second_dir_border_spread, second_dir_small_solver, speed_factor_ln_reference, kelvin_exponent_each, arrhenius_energy_kelvin, consumed_species_flags, stoich_net_shift, boundary_supplying_volume, boundary_target_volume, boundary_slot_used, boundary_transfer_weight, open_volume_flags):
    contra_x = grid_stretch_main[0] * motion_components[0] + grid_stretch_cross[0] * motion_components[1]
    contra_y = grid_stretch_cross[1] * motion_components[0] + grid_stretch_main[1] * motion_components[1]
    flux_x = contra_x[None] * species_partial_mass
    flux_y = contra_y[None] * species_partial_mass

    lines_x = flux_x.reshape(NS, VOLUMES_ALONG_U, N_GX, CX, VOLUMES_ALONG_N)
    local_x = jnp.einsum('ab,nzjby->nzjay', first_dir_piece_solver, lines_x, precision=HI)
    side_x = jnp.einsum('kb,nzjby->nzjky', first_dir_rhs_condense, lines_x, precision=HI).reshape(NS, VOLUMES_ALONG_U, KX, VOLUMES_ALONG_N)
    solved_x = jnp.einsum('ij,nzjy->nziy', first_dir_small_solver, side_x, precision=HI).reshape(NS, VOLUMES_ALONG_U, N_GX, K, VOLUMES_ALONG_N)
    deriv_x = (local_x + jnp.einsum('ak,nzjky->nzjay', first_dir_border_spread, solved_x, precision=HI)).reshape(NS, VOLUMES_ALONG_U, VOLUMES_ALONG_E, VOLUMES_ALONG_N)

    lines_y = flux_y.reshape(NS, VOLUMES_ALONG_U, VOLUMES_ALONG_E, N_GY, CY)
    local_y = jnp.einsum('ab,nzxjb->nzxja', second_dir_piece_solver, lines_y, precision=HI)
    side_y = jnp.einsum('kb,nzxjb->nzxjk', second_dir_rhs_condense, lines_y, precision=HI).reshape(NS, VOLUMES_ALONG_U, VOLUMES_ALONG_E, KY)
    solved_y = jnp.einsum('ij,nzxj->nzxi', second_dir_small_solver, side_y, precision=HI).reshape(NS, VOLUMES_ALONG_U, VOLUMES_ALONG_E, N_GY, K)
    deriv_y = (local_y + jnp.einsum('ak,nzxjk->nzxja', second_dir_border_spread, solved_y, precision=HI)).reshape(NS, VOLUMES_ALONG_U, VOLUMES_ALONG_E, VOLUMES_ALONG_N)

    kelvin_natural_ln = jnp.log(kelvin_field / 1500.0)
    reciprocal_kelvin = 1.0 / kelvin_field - 1.0 / 1500.0
    natural_speed_exponent = speed_factor_ln_reference[:, None, None, None] + kelvin_exponent_each[:, None, None, None] * kelvin_natural_ln[None] - arrhenius_energy_kelvin[:, None, None, None] * reciprocal_kelvin[None]
    log_conc = jnp.log(species_partial_mass)
    progress = jnp.exp(natural_speed_exponent + jnp.einsum('rn,nzxy->rzxy', consumed_species_flags.astype(jnp.float32), log_conc, precision=HI))
    source = 0.2 * jnp.einsum('rn,rzxy->nzxy', stoich_net_shift.astype(jnp.float32), progress, precision=HI)

    blocks = to_blocks(species_partial_mass)
    source_cells = boundary_supplying_volume.reshape(N_GX * N_GY * N_GZ, FMAX)
    target_cells = boundary_target_volume.reshape(N_GX * N_GY * N_GZ, FMAX)
    weight = (boundary_transfer_weight * boundary_slot_used.astype(jnp.float32)).reshape(N_GX * N_GY * N_GZ, FMAX)
    picked = jax.vmap(lambda blk, idx: blk[:, idx])(blocks, source_cells)
    outgoing = picked * weight[:, None, :]
    incoming = outgoing.reshape(N_GX * N_GY, N_GZ, NS, FMAX)[:, ::-1].reshape(N_GX * N_GY * N_GZ, NS, FMAX)
    wall = from_blocks(jax.vmap(wall_block)(source_cells, target_cells, outgoing, incoming))

    section_rhs = open_volume_flags.astype(jnp.float32)[None] * (source + wall - volume_scaling_reciprocal[None] * (deriv_x + deriv_y))
    section_state = species_partial_mass + 0.25 * section_rhs
    return section_rhs, section_state
```

```python
import functools

import jax
import jax.numpy as jnp
from jax import lax
from jax.experimental import pallas as pl
from jax.experimental.pallas import tpu as pltpu
from jax.sharding import PartitionSpec as P

HI = lax.Precision.HIGHEST
F32 = jnp.float32
B16 = jnp.bfloat16
MESH = pl.DeviceIdType.MESH
LANES = 128


def shift_of(n):
    assert n & (n - 1) == 0
    return n.bit_length() - 1


def over(value, n):
    return lax.shift_right_logical(value, jnp.int32(shift_of(n)))


def rest(value, n):
    return value & (n - 1)


def iota(shape, dim):
    return lax.broadcasted_iota(jnp.int32, shape, dim)


def ones_where(mask):
    return jnp.where(mask, F32(1), F32(0))


def fdot(a, b):
    return jnp.dot(a, b, precision=HI, preferred_element_type=F32)


def bdot(a, b):
    return jnp.dot(a, b, preferred_element_type=F32)


def split(value):
    high = value.astype(B16)
    return high, (value - high.astype(F32)).astype(B16)


def dot3(a, b):
    return bdot(a[0], b[0]) + bdot(a[0], b[1]) + bdot(a[1], b[0])


def dot2(a, b):
    return bdot(a, b[0]) + bdot(a, b[1])


def kernel(
    n_gx,
    n_gy,
    rows_x,
    sp,
    motion,
    g_main,
    g_cross,
    vol,
    kelvin,
    dx,
    cx,
    bx,
    mx,
    dy,
    cy,
    by,
    my,
    ln_ref,
    kexp,
    energy,
    flags,
    stoich,
    supply,
    target,
    used,
    weight,
    q,
    ex_all,
    ey_all,
    wall_out,
    wall_in,
    fx_h,
    fx_l,
    fy_h,
    fy_l,
    u_h,
    u_l,
    acc,
    x_send,
    x_recv,
    y_send,
    y_recv,
    w_send,
    w_recv,
):
    species, rows, lanes = sp.shape
    planes = rows // rows_x
    unknowns = cx.shape[0]
    slots = supply.shape[1]
    reactions = flags.shape[0]
    padded = ey_all.shape[1]
    me_x, me_y, me_z = lax.axis_index("gx"), lax.axis_index("gy"), lax.axis_index("gz")

    def along_x(d):
        return {"gx": lax.rem(me_x + d, n_gx)}

    def along_y(d):
        return {"gy": lax.rem(me_y + d, n_gy)}

    across = {"gz": 1 - me_z}

    barrier = pltpu.get_barrier_semaphore()
    for d in range(1, n_gx):
        pl.semaphore_signal(barrier, inc=1, device_id=along_x(d), device_id_type=MESH)
    for d in range(1, n_gy):
        pl.semaphore_signal(barrier, inc=1, device_id=along_y(d), device_id_type=MESH)
    pl.semaphore_signal(barrier, inc=1, device_id=across, device_id_type=MESH)

    def part(s):
        return slice(s * lanes, (s + 1) * lanes)

    contra_x = g_main[0] * motion[0] + g_cross[0] * motion[1]
    for s in range(species):
        fx_h[:, part(s)], fx_l[:, part(s)] = split(contra_x * sp[s])
    pick = ones_where(rest(iota((rows, rows_x), 0), rows_x) == iota((rows, rows_x), 1))
    pick_t = ones_where(rest(iota((rows_x, rows), 1), rows_x) == iota((rows_x, rows), 0))
    side = unknowns * planes
    sel = ones_where(over(iota((side, unknowns), 0), planes) == iota((side, unknowns), 1))
    cx_big = jnp.where(
        rest(iota((side, rows), 0), planes) == over(iota((side, rows), 1), rows_x),
        fdot(fdot(sel, cx[...]), pick_t),
        F32(0),
    )
    ex_all[me_x] = dot3(split(cx_big), (fx_h[...], fx_l[...]))
    pl.semaphore_wait(barrier, n_gx + n_gy - 1)
    x_copies = []
    for d in range(1, n_gx):
        copy = pltpu.make_async_remote_copy(
            src_ref=ex_all.at[me_x],
            dst_ref=ex_all.at[me_x],
            send_sem=x_send.at[d],
            recv_sem=x_recv.at[d],
            device_id=along_x(d),
            device_id_type=MESH,
        )
        copy.start()
        x_copies.append(copy)

    contra_y = g_cross[1] * motion[0] + g_main[1] * motion[1]
    for s in range(species):
        fy_h[:, part(s)], fy_l[:, part(s)] = split(contra_y * sp[s])
    sel = ones_where(rest(iota((lanes, unknowns), 0), unknowns) == iota((lanes, unknowns), 1))
    cy_t = fdot(sel, cy[...]).T
    owner = over(iota((lanes, lanes), 1), unknowns)
    cy_h, cy_l = split(
        jnp.concatenate([jnp.where(owner == s, cy_t, F32(0)) for s in range(species)], axis=0)
    )
    ey = dot3((fy_h[...], fy_l[...]), (cy_h, cy_l))
    ey_all[me_y] = ey.T[:padded]
    y_copies = []
    for d in range(1, n_gy):
        copy = pltpu.make_async_remote_copy(
            src_ref=ey_all.at[me_y],
            dst_ref=ey_all.at[me_y],
            send_sem=y_send.at[d],
            recv_sem=y_recv.at[d],
            device_id=along_y(d),
            device_id_type=MESH,
        )
        copy.start()
        y_copies.append(copy)

    def down(row):
        return jnp.broadcast_to(row, (lanes, slots)).T

    supply_col = down(supply[...])
    carried = down(weight[...] * used[...].astype(F32))
    wide = jnp.concatenate([over(supply_col, lanes)] * (rows // lanes), axis=1)
    from_rows = ones_where(wide == iota((slots, rows), 1)).astype(B16)
    from_lane = rest(supply_col, lanes) == iota((slots, lanes), 1)
    for s in range(species):
        u_h[:, part(s)], u_l[:, part(s)] = split(sp[s])
    gathered = dot2(from_rows, (u_h[...], u_l[...]))
    lane = iota((slots, lanes), 1)
    sent = jnp.zeros((slots, lanes), F32)
    for s in range(species):
        kept = jnp.where(from_lane, gathered[:, part(s)] * carried, F32(0))
        u_h[:, part(s)], u_l[:, part(s)] = split(-kept)
        sent = jnp.where(lane == s, jnp.sum(kept, axis=1, keepdims=True), sent)
    wall_out[...] = sent
    w_copy = pltpu.make_async_remote_copy(
        src_ref=wall_out,
        dst_ref=wall_in,
        send_sem=w_send,
        recv_sem=w_recv,
        device_id=across,
        device_id_type=MESH,
    )
    w_copy.start()

    chunk = 16

    def chemistry(i, carry):
        at = pl.ds(pl.multiple_of(i * chunk, chunk), chunk)
        temperature = kelvin[at, :]
        ln_t = jnp.log(temperature / F32(1500.0))
        rec_t = F32(1.0) / temperature - F32(1.0 / 1500.0)
        logs = [jnp.log(sp[s, at, :]) for s in range(species)]
        sums = [jnp.zeros((chunk, lanes), F32) for _ in range(species)]
        for r in range(reactions):
            value = ln_ref[r] + kexp[r] * ln_t - energy[r] * rec_t
            for s in range(species):
                value = value + flags[r, s].astype(F32) * logs[s]
            progress = jnp.exp(value)
            for s in range(species):
                sums[s] = sums[s] + stoich[r, s].astype(F32) * progress
        for s in range(species):
            q[s, at, :] = F32(0.2) * sums[s]
        return carry

    lax.fori_loop(0, rows // chunk, chemistry, 0)

    same = over(iota((rows, rows), 0), rows_x) == over(iota((rows, rows), 1), rows_x)
    dx_big = jnp.where(same, fdot(fdot(pick, dx[...]), pick_t), F32(0))
    acc[...] = dot3(split(dx_big), (fx_h[...], fx_l[...]))
    dy_t = split(dy[...].T)
    for s in range(species):
        acc[:, part(s)] += dot3((fy_h[:, part(s)], fy_l[:, part(s)]), dy_t)

    to_supply = ones_where(
        over(jnp.broadcast_to(supply[...], (rows, slots)), lanes) == iota((rows, slots), 0)
    ).astype(B16)
    to_target = ones_where(
        over(jnp.broadcast_to(target[...], (rows, slots)), lanes) == iota((rows, slots), 0)
    ).astype(B16)
    own_wall = dot2(to_supply, (u_h[...], u_l[...]))
    for s in range(species):
        q[s] += own_wall[:, part(s)]
    to_lane = rest(down(target[...]), lanes) == lane
    w_copy.wait_recv()
    incoming = wall_in[...]
    for s in range(species):
        spread = jnp.broadcast_to(incoming[:, s : s + 1], (slots, lanes))
        u_h[:, part(s)], u_l[:, part(s)] = split(jnp.where(to_lane, spread, F32(0)))
    far_wall = dot2(to_target, (u_h[...], u_l[...]))
    for s in range(species):
        q[s] += far_wall[:, part(s)]

    wy = fdot(by[...], my[...])
    pieces = []
    for i in range(n_gy):
        shape = (padded, n_gy * unknowns)
        sel = ones_where(rest(iota(shape, 0), unknowns) + i * unknowns == iota(shape, 1))
        pieces.append(
            lax.dot_general(
                sel, wy, (((1,), (1,)), ((), ())), precision=HI, preferred_element_type=F32
            )
        )
    base = jnp.concatenate(pieces, axis=0)
    owner = jnp.concatenate([over(iota((padded, lanes), 0), unknowns)] * n_gy, axis=0)
    wy_big = jnp.concatenate(
        [jnp.where(owner == s, base, F32(0)) for s in range(species)], axis=1
    )
    for copy in y_copies:
        copy.wait_recv()
    ey = ey_all[...].reshape(n_gy * padded, rows).T
    acc[...] += dot3(split(ey), split(wy_big))

    count = n_gx * unknowns
    wide = count * planes
    sel = ones_where(over(iota((count, wide), 1), planes) == iota((count, wide), 0))
    wx = fdot(pick, fdot(fdot(bx[...], mx[...]), sel))
    wx_big = split(
        jnp.where(
            over(iota((rows, wide), 0), rows_x) == rest(iota((rows, wide), 1), planes), wx, F32(0)
        )
    )
    for copy in x_copies:
        copy.wait_recv()
    ex = split(ex_all[...].reshape(wide, species * lanes))
    total = acc[...] + dot3(wx_big, ex)
    for s in range(species):
        q[s] = q[s] - vol[...] * total[:, part(s)]

    for copy in x_copies + y_copies + [w_copy]:
        copy.wait_send()


def per_device(n_gx, n_gy, *args):
    species_partial_mass = args[0]
    open_volume_flags = args[-1]
    species, planes, rows_x, lanes = species_partial_mass.shape
    rows = planes * rows_x
    ins = [
        species_partial_mass.reshape(species, rows, lanes),
        *(a.reshape(2, rows, lanes) for a in args[1:4]),
        *(a.reshape(rows, lanes) for a in args[4:6]),
        *args[6:19],
        *(a.reshape(1, -1) for a in args[19:23]),
    ]
    slots = ins[-1].shape[1]
    unknowns = args[7].shape[0]
    padded = -(-species * unknowns // 16) * 16
    wide = species * lanes
    vmem = pl.BlockSpec(memory_space=pltpu.VMEM)
    smem = pl.BlockSpec(memory_space=pltpu.SMEM)
    q = pl.pallas_call(
        functools.partial(kernel, n_gx, n_gy, rows_x),
        out_shape=jax.ShapeDtypeStruct((species, rows, lanes), F32),
        in_specs=[vmem] * 14 + [smem] * 5 + [vmem] * 4,
        out_specs=vmem,
        scratch_shapes=[
            pltpu.VMEM((n_gx, unknowns * planes, wide), F32),
            pltpu.VMEM((n_gy, padded, rows), F32),
            pltpu.VMEM((slots, lanes), F32),
            pltpu.VMEM((slots, lanes), F32),
            *([pltpu.VMEM((rows, wide), B16)] * 4),
            *([pltpu.VMEM((max(rows, slots), wide), B16)] * 2),
            pltpu.VMEM((rows, wide), F32),
            pltpu.SemaphoreType.DMA((n_gx,)),
            pltpu.SemaphoreType.DMA((n_gx,)),
            pltpu.SemaphoreType.DMA((n_gy,)),
            pltpu.SemaphoreType.DMA((n_gy,)),
            pltpu.SemaphoreType.DMA,
            pltpu.SemaphoreType.DMA,
        ],
        compiler_params=pltpu.CompilerParams(
            collective_id=0, has_side_effects=True, vmem_limit_bytes=48 * 2**20
        ),
    )(*ins)
    q = q.reshape(species_partial_mass.shape)
    section_rhs = open_volume_flags.astype(F32)[None] * q
    section_state = species_partial_mass + 0.25 * section_rhs
    return (section_rhs, section_state)


def solution(mesh):
    grid = P(None, "gz", "gx", "gy")
    cells = P("gz", "gx", "gy")
    faces = P("gx", "gy", "gz")
    in_specs = (
        *([grid] * 4),
        *([cells] * 2),
        *([P()] * 3),
        P("gx", None),
        *([P()] * 3),
        P("gy", None),
        *([P()] * 5),
        *([faces] * 4),
        cells,
    )
    return jax.shard_map(
        functools.partial(per_device, mesh.shape["gx"], mesh.shape["gy"]),
        mesh=mesh,
        in_specs=in_specs,
        out_specs=(grid, grid),
        check_vma=False,
    )
```

```python
import functools

import jax
import jax.numpy as jnp
from jax import lax
from jax.experimental import pallas as pl
from jax.experimental.pallas import tpu as pltpu
from jax.sharding import PartitionSpec as P

HI = lax.Precision.HIGHEST
F32 = jnp.float32
B16 = jnp.bfloat16
MESH = pl.DeviceIdType.MESH
INS = 24


def shift_of(n):
    assert n & (n - 1) == 0
    return n.bit_length() - 1


def over(value, n):
    return lax.shift_right_logical(value, jnp.int32(shift_of(n)))


def rest(value, n):
    return value & (n - 1)


def iota(shape, dim):
    return lax.broadcasted_iota(jnp.int32, shape, dim)


def ones_where(mask):
    return jnp.where(mask, F32(1), F32(0))


def fdot(a, b):
    return jnp.dot(a, b, precision=HI, preferred_element_type=F32)


def fdot_t(a, b):
    return lax.dot_general(
        a, b, (((1,), (1,)), ((), ())), precision=HI, preferred_element_type=F32
    )


def bdot(a, b):
    return jnp.dot(a, b, preferred_element_type=F32)


def split(value):
    high = value.astype(B16)
    return high, (value - high.astype(F32)).astype(B16)


def dot3(a, b):
    return bdot(a[0], b[0]) + bdot(a[0], b[1]) + bdot(a[1], b[0])


def dot2(a, b):
    return bdot(a, b[0]) + bdot(a, b[1])


def kernel(
    n_gx,
    n_gy,
    rows_x,
    *refs,
):
    held = refs[-INS:]
    incoming_sem = refs[-INS - 1]
    (
        q,
        fluid_out,
        ex_all,
        ey_all,
        wall_out,
        wall_in,
        fx_h,
        fx_l,
        fy_h,
        fy_l,
        u_h,
        u_l,
        acc,
        x_send,
        x_recv,
        y_send,
        y_recv,
        w_send,
        w_recv,
    ) = refs[INS : -INS - 1]
    (
        sp,
        motion,
        g_main,
        g_cross,
        vol,
        kelvin,
        dx,
        cx,
        bx,
        mx,
        dy,
        cy,
        by,
        my,
        ln_ref,
        kexp,
        energy,
        flags,
        stoich,
        supply,
        target,
        used,
        weight,
        fluid,
    ) = held
    loads = {
        id(dst): pltpu.make_async_copy(src, dst, incoming_sem.at[i])
        for i, (src, dst) in enumerate(zip(refs[:INS], held))
    }
    first = (sp, motion, g_main, g_cross, cx, cy, supply, used, weight)
    for ref in first + tuple(ref for ref in held if all(ref is not other for other in first)):
        loads[id(ref)].start()

    def arrive(*some):
        for ref in some:
            loads[id(ref)].wait()

    species, rows, lanes = sp.shape
    planes = rows // rows_x
    unknowns = cx.shape[0]
    slots = supply.shape[1]
    reactions = flags.shape[1]
    padded = ey_all.shape[1]
    me_x, me_y, me_z = lax.axis_index("gx"), lax.axis_index("gy"), lax.axis_index("gz")

    def along_x(d):
        return {"gx": lax.rem(me_x + d, n_gx)}

    def along_y(d):
        return {"gy": lax.rem(me_y + d, n_gy)}

    across = {"gz": 1 - me_z}

    barrier = pltpu.get_barrier_semaphore()
    for d in range(1, n_gx):
        pl.semaphore_signal(barrier, inc=1, device_id=along_x(d), device_id_type=MESH)
    for d in range(1, n_gy):
        pl.semaphore_signal(barrier, inc=1, device_id=along_y(d), device_id_type=MESH)
    pl.semaphore_signal(barrier, inc=1, device_id=across, device_id_type=MESH)

    def part(s):
        return slice(s * lanes, (s + 1) * lanes)

    arrive(sp, motion, g_main, g_cross, cx)
    contra_x = g_main[0] * motion[0] + g_cross[0] * motion[1]
    for s in range(species):
        fx_h[:, part(s)], fx_l[:, part(s)] = split(contra_x * sp[s])
    pick = ones_where(rest(iota((rows, rows_x), 0), rows_x) == iota((rows, rows_x), 1))
    pick_t = ones_where(rest(iota((rows_x, rows), 1), rows_x) == iota((rows_x, rows), 0))
    side = unknowns * planes
    sel = ones_where(over(iota((side, unknowns), 0), planes) == iota((side, unknowns), 1))
    cx_big = jnp.where(
        rest(iota((side, rows), 0), planes) == over(iota((side, rows), 1), rows_x),
        fdot(fdot(sel, cx[...]), pick_t),
        F32(0),
    )
    ex_all[me_x] = dot3(split(cx_big), (fx_h[...], fx_l[...]))
    pl.semaphore_wait(barrier, n_gx + n_gy - 1)
    x_copies = []
    for d in range(1, n_gx):
        copy = pltpu.make_async_remote_copy(
            src_ref=ex_all.at[me_x],
            dst_ref=ex_all.at[me_x],
            send_sem=x_send.at[d],
            recv_sem=x_recv.at[d],
            device_id=along_x(d),
            device_id_type=MESH,
        )
        copy.start()
        x_copies.append(copy)

    contra_y = g_cross[1] * motion[0] + g_main[1] * motion[1]
    for s in range(species):
        fy_h[:, part(s)], fy_l[:, part(s)] = split(contra_y * sp[s])
    sel = ones_where(rest(iota((lanes, unknowns), 0), unknowns) == iota((lanes, unknowns), 1))
    arrive(cy)
    cy_t = fdot(sel, cy[...]).T
    owner = over(iota((lanes, lanes), 1), unknowns)
    cy_h, cy_l = split(
        jnp.concatenate([jnp.where(owner == s, cy_t, F32(0)) for s in range(species)], axis=0)
    )
    ey = dot3((fy_h[...], fy_l[...]), (cy_h, cy_l))
    ey_all[me_y] = ey.T[:padded]
    y_copies = []
    for d in range(1, n_gy):
        copy = pltpu.make_async_remote_copy(
            src_ref=ey_all.at[me_y],
            dst_ref=ey_all.at[me_y],
            send_sem=y_send.at[d],
            recv_sem=y_recv.at[d],
            device_id=along_y(d),
            device_id_type=MESH,
        )
        copy.start()
        y_copies.append(copy)

    def down(row):
        return jnp.broadcast_to(row, (lanes, slots)).T

    arrive(supply, used, weight)
    supply_col = down(supply[...])
    carried = down(weight[...] * used[...].astype(F32))
    wide = jnp.concatenate([over(supply_col, lanes)] * (rows // lanes), axis=1)
    from_rows = ones_where(wide == iota((slots, rows), 1)).astype(B16)
    from_lane = rest(supply_col, lanes) == iota((slots, lanes), 1)
    for s in range(species):
        u_h[:, part(s)], u_l[:, part(s)] = split(sp[s])
    gathered = dot2(from_rows, (u_h[...], u_l[...]))
    lane = iota((slots, lanes), 1)
    sent = jnp.zeros((slots, lanes), F32)
    for s in range(species):
        kept = jnp.where(from_lane, gathered[:, part(s)] * carried, F32(0))
        u_h[:, part(s)], u_l[:, part(s)] = split(-kept)
        sent = jnp.where(lane == s, jnp.sum(kept, axis=1, keepdims=True), sent)
    wall_out[...] = sent
    w_copy = pltpu.make_async_remote_copy(
        src_ref=wall_out,
        dst_ref=wall_in,
        send_sem=w_send,
        recv_sem=w_recv,
        device_id=across,
        device_id_type=MESH,
    )
    w_copy.start()

    chunk = 16
    arrive(kelvin, ln_ref, kexp, energy, flags, stoich)

    def chemistry(i, carry):
        at = pl.ds(pl.multiple_of(i * chunk, chunk), chunk)
        temperature = kelvin[at, :]
        ln_t = jnp.log(temperature / F32(1500.0))
        rec_t = F32(1.0) / temperature - F32(1.0 / 1500.0)
        logs = [jnp.log(sp[s, at, :]) for s in range(species)]
        sums = [jnp.zeros((chunk, lanes), F32) for _ in range(species)]
        for r in range(reactions):
            value = ln_ref[r] + kexp[r] * ln_t - energy[r] * rec_t
            for s in range(species):
                value = value + flags[s, r].astype(F32) * logs[s]
            progress = jnp.exp(value)
            for s in range(species):
                sums[s] = sums[s] + stoich[s, r].astype(F32) * progress
        for s in range(species):
            q[s, at, :] = F32(0.2) * sums[s]
        return carry

    lax.fori_loop(0, rows // chunk, chemistry, 0)

    arrive(dx, dy, target, vol, bx, mx, by, my, fluid)
    fluid_out[...] = fluid[...].astype(F32)
    same = over(iota((rows, rows), 0), rows_x) == over(iota((rows, rows), 1), rows_x)
    dx_big = jnp.where(same, fdot(fdot(pick, dx[...]), pick_t), F32(0))
    acc[...] = dot3(split(dx_big), (fx_h[...], fx_l[...]))
    dy_t = split(dy[...].T)
    for s in range(species):
        acc[:, part(s)] += dot3((fy_h[:, part(s)], fy_l[:, part(s)]), dy_t)

    to_supply = ones_where(
        over(jnp.broadcast_to(supply[...], (rows, slots)), lanes) == iota((rows, slots), 0)
    ).astype(B16)
    to_target = ones_where(
        over(jnp.broadcast_to(target[...], (rows, slots)), lanes) == iota((rows, slots), 0)
    ).astype(B16)
    own_wall = dot2(to_supply, (u_h[...], u_l[...]))
    for s in range(species):
        q[s] += own_wall[:, part(s)]
    to_lane = rest(down(target[...]), lanes) == lane
    w_copy.wait_recv()
    incoming = wall_in[...]
    for s in range(species):
        spread = jnp.broadcast_to(incoming[:, s : s + 1], (slots, lanes))
        u_h[:, part(s)], u_l[:, part(s)] = split(jnp.where(to_lane, spread, F32(0)))
    far_wall = dot2(to_target, (u_h[...], u_l[...]))
    for s in range(species):
        q[s] += far_wall[:, part(s)]

    pieces = []
    for i in range(n_gy):
        shape = (padded, n_gy * unknowns)
        sel = ones_where(rest(iota(shape, 0), unknowns) + i * unknowns == iota(shape, 1))
        pieces.append(fdot(fdot_t(sel, my[...]), by[...]))
    base = jnp.concatenate(pieces, axis=0)
    owner = jnp.concatenate([over(iota((padded, lanes), 0), unknowns)] * n_gy, axis=0)
    wy_big = jnp.concatenate(
        [jnp.where(owner == s, base, F32(0)) for s in range(species)], axis=1
    )
    for copy in y_copies:
        copy.wait_recv()
    ey = ey_all[...].reshape(n_gy * padded, rows).T
    acc[...] += dot3(split(ey), split(wy_big))

    count = n_gx * unknowns
    wide = count * planes
    sel = ones_where(over(iota((count, wide), 1), planes) == iota((count, wide), 0))
    wx = fdot(fdot_t(pick, bx[...]), fdot(mx[...], sel))
    wx_big = split(
        jnp.where(
            over(iota((rows, wide), 0), rows_x) == rest(iota((rows, wide), 1), planes), wx, F32(0)
        )
    )
    for copy in x_copies:
        copy.wait_recv()
    ex = split(ex_all[...].reshape(wide, species * lanes))
    total = acc[...] + dot3(wx_big, ex)
    for s in range(species):
        q[s] = q[s] - vol[...] * total[:, part(s)]

    for copy in x_copies + y_copies + [w_copy]:
        copy.wait_send()


def per_device(n_gx, n_gy, *args):
    species_partial_mass = args[0]
    species, planes, rows_x, lanes = species_partial_mass.shape
    rows = planes * rows_x
    ins = [
        species_partial_mass.reshape(species, rows, lanes),
        *(a.reshape(2, rows, lanes) for a in args[1:4]),
        *(a.reshape(rows, lanes) for a in args[4:6]),
        *args[6:8],
        args[8].T,
        *args[9:12],
        args[12].T,
        *args[13:17],
        args[17].T,
        args[18].T,
        *(a.reshape(1, -1) for a in args[19:23]),
        args[23].reshape(rows, lanes),
    ]
    slots = ins[-2].shape[1]
    unknowns = args[7].shape[0]
    padded = -(-species * unknowns // 16) * 16
    wide = species * lanes
    spaces = [pltpu.VMEM] * 14 + [pltpu.SMEM] * 5 + [pltpu.VMEM] * 5
    q, fluid = pl.pallas_call(
        functools.partial(kernel, n_gx, n_gy, rows_x),
        out_shape=(
            jax.ShapeDtypeStruct((species, rows, lanes), F32),
            jax.ShapeDtypeStruct((rows, lanes), F32),
        ),
        in_specs=[pl.BlockSpec(memory_space=pl.ANY)] * INS,
        out_specs=[pl.BlockSpec(memory_space=pltpu.VMEM)] * 2,
        scratch_shapes=[
            pltpu.VMEM((n_gx, unknowns * planes, wide), F32),
            pltpu.VMEM((n_gy, padded, rows), F32),
            pltpu.VMEM((slots, lanes), F32),
            pltpu.VMEM((slots, lanes), F32),
            *([pltpu.VMEM((rows, wide), B16)] * 4),
            *([pltpu.VMEM((max(rows, slots), wide), B16)] * 2),
            pltpu.VMEM((rows, wide), F32),
            pltpu.SemaphoreType.DMA((n_gx,)),
            pltpu.SemaphoreType.DMA((n_gx,)),
            pltpu.SemaphoreType.DMA((n_gy,)),
            pltpu.SemaphoreType.DMA((n_gy,)),
            pltpu.SemaphoreType.DMA,
            pltpu.SemaphoreType.DMA,
            pltpu.SemaphoreType.DMA((INS,)),
            *(space(a.shape, a.dtype) for space, a in zip(spaces, ins)),
        ],
        compiler_params=pltpu.CompilerParams(
            collective_id=0, has_side_effects=True, vmem_limit_bytes=56 * 2**20
        ),
    )(*ins)
    q = q.reshape(species_partial_mass.shape)
    section_rhs = fluid.reshape(planes, rows_x, lanes)[None] * q
    section_state = species_partial_mass + 0.25 * section_rhs
    return (section_rhs, section_state)


def solution(mesh):
    grid = P(None, "gz", "gx", "gy")
    cells = P("gz", "gx", "gy")
    faces = P("gx", "gy", "gz")
    in_specs = (
        *([grid] * 4),
        *([cells] * 2),
        *([P()] * 3),
        P("gx", None),
        *([P()] * 3),
        P("gy", None),
        *([P()] * 5),
        *([faces] * 4),
        cells,
    )
    return jax.shard_map(
        functools.partial(per_device, mesh.shape["gx"], mesh.shape["gy"]),
        mesh=mesh,
        in_specs=in_specs,
        out_specs=(grid, grid),
        check_vma=False,
    )
```

```python
import functools

import jax
import jax.numpy as jnp
from jax import lax
from jax.experimental import pallas as pl
from jax.experimental.pallas import tpu as pltpu
from jax.sharding import PartitionSpec as P

HI = lax.Precision.HIGHEST
F32 = jnp.float32
B16 = jnp.bfloat16
MESH = pl.DeviceIdType.MESH
INS = 24
GROUP = 8


def shift_of(n):
    assert n & (n - 1) == 0
    return n.bit_length() - 1


def over(value, n):
    return lax.shift_right_logical(value, jnp.int32(shift_of(n)))


def rest(value, n):
    return value & (n - 1)


def iota(shape, dim):
    return lax.broadcasted_iota(jnp.int32, shape, dim)


def ones_where(mask):
    return jnp.where(mask, F32(1), F32(0))


def fdot(a, b):
    return jnp.dot(a, b, precision=HI, preferred_element_type=F32)


def fdot_t(a, b):
    return lax.dot_general(
        a, b, (((1,), (1,)), ((), ())), precision=HI, preferred_element_type=F32
    )


def bdot(a, b):
    return jnp.dot(a, b, preferred_element_type=F32)


def split(value):
    high = value.astype(B16)
    return high, (value - high.astype(F32)).astype(B16)


def dot3(a, b):
    return bdot(a[0], b[0]) + bdot(a[0], b[1]) + bdot(a[1], b[0])


def dot2(a, b):
    return bdot(a, b[0]) + bdot(a, b[1])


def kernel(
    n_gx,
    n_gy,
    rows_x,
    *refs,
):
    held = refs[-INS:]
    incoming_sem = refs[-INS - 1]
    (
        q,
        fluid_out,
        ex_all,
        ey_all,
        wall_out,
        wall_in,
        fx_h,
        fx_l,
        fy_h,
        fy_l,
        u_h,
        u_l,
        acc,
        x_send,
        x_recv,
        y_send,
        y_recv,
        w_send,
        w_recv,
    ) = refs[INS : -INS - 1]
    (
        sp,
        motion,
        g_main,
        g_cross,
        vol,
        kelvin,
        dx,
        cx,
        bx,
        mx,
        dy,
        cy,
        by,
        my,
        ln_ref,
        kexp,
        energy,
        flags,
        stoich,
        supply,
        target,
        used,
        weight,
        fluid,
    ) = held
    loads = {
        id(dst): pltpu.make_async_copy(src, dst, incoming_sem.at[i])
        for i, (src, dst) in enumerate(zip(refs[:INS], held))
    }
    first = (sp, motion, g_main, g_cross, cx, cy, supply, used, weight)
    for ref in first + tuple(ref for ref in held if all(ref is not other for other in first)):
        loads[id(ref)].start()

    def arrive(*some):
        for ref in some:
            loads[id(ref)].wait()

    species, rows, lanes = sp.shape
    planes = rows // rows_x
    unknowns = cx.shape[0]
    slots = supply.shape[1]
    reactions = flags.shape[1]
    padded = ey_all.shape[1]
    me_x, me_y, me_z = lax.axis_index("gx"), lax.axis_index("gy"), lax.axis_index("gz")

    def along_x(d):
        return {"gx": lax.rem(me_x + d, n_gx)}

    def along_y(d):
        return {"gy": lax.rem(me_y + d, n_gy)}

    across = {"gz": 1 - me_z}

    barrier = pltpu.get_barrier_semaphore()
    for d in range(1, n_gx):
        pl.semaphore_signal(barrier, inc=1, device_id=along_x(d), device_id_type=MESH)
    for d in range(1, n_gy):
        pl.semaphore_signal(barrier, inc=1, device_id=along_y(d), device_id_type=MESH)
    pl.semaphore_signal(barrier, inc=1, device_id=across, device_id_type=MESH)

    def part(s):
        return slice(s * lanes, (s + 1) * lanes)

    arrive(sp, motion, g_main, g_cross, cx)
    contra_x = g_main[0] * motion[0] + g_cross[0] * motion[1]
    for s in range(species):
        fx_h[:, part(s)], fx_l[:, part(s)] = split(contra_x * sp[s])
    pick = ones_where(rest(iota((rows, rows_x), 0), rows_x) == iota((rows, rows_x), 1))
    pick_t = ones_where(rest(iota((rows_x, rows), 1), rows_x) == iota((rows_x, rows), 0))
    side = unknowns * planes
    sel = ones_where(over(iota((side, unknowns), 0), planes) == iota((side, unknowns), 1))
    cx_big = jnp.where(
        rest(iota((side, rows), 0), planes) == over(iota((side, rows), 1), rows_x),
        fdot(fdot(sel, cx[...]), pick_t),
        F32(0),
    )
    ex_all[me_x] = dot3(split(cx_big), (fx_h[...], fx_l[...]))
    pl.semaphore_wait(barrier, n_gx + n_gy - 1)
    x_copies = []
    for d in range(1, n_gx):
        copy = pltpu.make_async_remote_copy(
            src_ref=ex_all.at[me_x],
            dst_ref=ex_all.at[me_x],
            send_sem=x_send.at[d],
            recv_sem=x_recv.at[d],
            device_id=along_x(d),
            device_id_type=MESH,
        )
        copy.start()
        x_copies.append(copy)

    contra_y = g_cross[1] * motion[0] + g_main[1] * motion[1]
    for s in range(species):
        fy_h[:, part(s)], fy_l[:, part(s)] = split(contra_y * sp[s])
    sel = ones_where(rest(iota((lanes, unknowns), 0), unknowns) == iota((lanes, unknowns), 1))
    arrive(cy)
    cy_t = fdot(sel, cy[...]).T
    owner = over(iota((lanes, lanes), 1), unknowns)
    cy_h, cy_l = split(
        jnp.concatenate([jnp.where(owner == s, cy_t, F32(0)) for s in range(species)], axis=0)
    )
    both = bdot(fy_h[...], jnp.concatenate([cy_h, cy_l], axis=1))
    ey = both[:, :lanes] + both[:, lanes:] + bdot(fy_l[...], cy_h)
    ey_all[me_y] = ey.T[:padded]
    y_copies = []
    for d in range(1, n_gy):
        copy = pltpu.make_async_remote_copy(
            src_ref=ey_all.at[me_y],
            dst_ref=ey_all.at[me_y],
            send_sem=y_send.at[d],
            recv_sem=y_recv.at[d],
            device_id=along_y(d),
            device_id_type=MESH,
        )
        copy.start()
        y_copies.append(copy)

    def down(row):
        return jnp.broadcast_to(row, (lanes, slots)).T

    arrive(supply, used, weight)
    supply_col = down(supply[...])
    carried = down(weight[...] * used[...].astype(F32))
    wide = jnp.concatenate([over(supply_col, lanes)] * (rows // lanes), axis=1)
    from_rows = ones_where(wide == iota((slots, rows), 1)).astype(B16)
    from_lane = rest(supply_col, lanes) == iota((slots, lanes), 1)
    for s in range(species):
        u_h[:, part(s)], u_l[:, part(s)] = split(sp[s])
    gathered = dot2(from_rows, (u_h[...], u_l[...]))
    lane = iota((slots, lanes), 1)
    sent = jnp.zeros((slots, lanes), F32)
    for s in range(species):
        kept = jnp.where(from_lane, gathered[:, part(s)] * carried, F32(0))
        u_h[:, part(s)], u_l[:, part(s)] = split(-kept)
        sent = jnp.where(lane == s, jnp.sum(kept, axis=1, keepdims=True), sent)
    wall_out[...] = sent
    w_copy = pltpu.make_async_remote_copy(
        src_ref=wall_out,
        dst_ref=wall_in,
        send_sem=w_send,
        recv_sem=w_recv,
        device_id=across,
        device_id_type=MESH,
    )
    w_copy.start()

    arrive(kelvin, ln_ref, kexp, energy, flags, stoich)
    high, deep = reactions * GROUP, species * GROUP
    sel_r = ones_where(over(iota((high, reactions), 0), GROUP) == iota((high, reactions), 1))
    sel_s = ones_where(over(iota((species, deep), 1), GROUP) == iota((species, deep), 0))
    consumed = jnp.where(
        rest(iota((high, deep), 0), GROUP) == rest(iota((high, deep), 1), GROUP),
        fdot(fdot_t(sel_r, flags[...].astype(F32)), sel_s),
        F32(0),
    )
    sel_s = ones_where(over(iota((deep, species), 0), GROUP) == iota((deep, species), 1))
    sel_r_t = ones_where(over(iota((reactions, high), 1), GROUP) == iota((reactions, high), 0))
    shifts = jnp.where(
        rest(iota((deep, high), 0), GROUP) == rest(iota((deep, high), 1), GROUP),
        fdot(fdot(sel_s, stoich[...].astype(F32)), sel_r_t),
        F32(0),
    ).astype(B16)

    def pieces_of(value):
        top = value.astype(B16).astype(F32)
        return top, value - top

    def each_reaction(row):
        column = jnp.sum(sel_r * row, axis=1, keepdims=True)
        return pieces_of(
            jnp.where(
                rest(iota((high, GROUP), 0), GROUP) == iota((high, GROUP), 1), column, F32(0)
            )
        )

    k_h, k_l = each_reaction(kexp[...])
    e_h, e_l = each_reaction(-energy[...])
    a_h, a_l = each_reaction(ln_ref[...])
    exponents = jnp.concatenate(
        [consumed, consumed, k_h, k_h, k_l, e_h, e_h, e_l, a_h, a_l], axis=1
    ).astype(B16)
    groups = 8
    chunk = groups * GROUP

    def side_by_side(value):
        return jnp.concatenate(
            [value[g * GROUP : (g + 1) * GROUP] for g in range(groups)], axis=1
        )

    def chemistry(i, carry):
        at = pl.ds(pl.multiple_of(i * chunk, chunk), chunk)
        temperature = side_by_side(kelvin[at, :])
        t_h, t_l = pieces_of(jnp.log(temperature / F32(1500.0)))
        r_h, r_l = pieces_of(F32(1.0) / temperature - F32(1.0 / 1500.0))
        logs = [pieces_of(jnp.log(side_by_side(sp[s, at, :]))) for s in range(species)]
        one = jnp.ones_like(temperature)
        stacked = jnp.concatenate(
            [x[0] for x in logs]
            + [x[1] for x in logs]
            + [t_h, t_l, t_h, r_h, r_l, r_h, one, one],
            axis=0,
        ).astype(B16)
        progress = jnp.exp(bdot(exponents, stacked))
        made = F32(0.2) * dot2(shifts, split(progress))
        for s in range(species):
            row = made[s * GROUP : (s + 1) * GROUP]
            q[s, at, :] = jnp.concatenate([row[:, part(g)] for g in range(groups)], axis=0)
        return carry

    lax.fori_loop(0, rows // chunk, chemistry, 0)

    arrive(dx, dy, target, vol, bx, mx, by, my, fluid)
    fluid_out[...] = fluid[...].astype(F32)
    same = over(iota((rows, rows), 0), rows_x) == over(iota((rows, rows), 1), rows_x)
    dx_big = jnp.where(same, fdot(fdot(pick, dx[...]), pick_t), F32(0))
    acc[...] = dot3(split(dx_big), (fx_h[...], fx_l[...]))
    dy_h, dy_l = split(dy[...].T)
    dy_two = jnp.concatenate(
        [
            jnp.concatenate([dy_h, dy_h], axis=0),
            jnp.concatenate([dy_l, jnp.zeros_like(dy_l)], axis=0),
        ],
        axis=1,
    )
    for s in range(species):
        both = bdot(jnp.concatenate([fy_h[:, part(s)], fy_l[:, part(s)]], axis=1), dy_two)
        acc[:, part(s)] += both[:, :lanes] + both[:, lanes:]

    to_supply = ones_where(
        over(jnp.broadcast_to(supply[...], (rows, slots)), lanes) == iota((rows, slots), 0)
    ).astype(B16)
    to_target = ones_where(
        over(jnp.broadcast_to(target[...], (rows, slots)), lanes) == iota((rows, slots), 0)
    ).astype(B16)
    own_wall = dot2(to_supply, (u_h[...], u_l[...]))
    for s in range(species):
        q[s] += own_wall[:, part(s)]
    to_lane = rest(down(target[...]), lanes) == lane
    w_copy.wait_recv()
    incoming = wall_in[...]
    for s in range(species):
        spread = jnp.broadcast_to(incoming[:, s : s + 1], (slots, lanes))
        u_h[:, part(s)], u_l[:, part(s)] = split(jnp.where(to_lane, spread, F32(0)))
    far_wall = dot2(to_target, (u_h[...], u_l[...]))
    for s in range(species):
        q[s] += far_wall[:, part(s)]

    pieces = []
    for i in range(n_gy):
        shape = (padded, n_gy * unknowns)
        sel = ones_where(rest(iota(shape, 0), unknowns) + i * unknowns == iota(shape, 1))
        pieces.append(fdot(fdot_t(sel, my[...]), by[...]))
    base = jnp.concatenate(pieces, axis=0)
    owner = jnp.concatenate([over(iota((padded, lanes), 0), unknowns)] * n_gy, axis=0)
    wy_big = jnp.concatenate(
        [jnp.where(owner == s, base, F32(0)) for s in range(species)], axis=1
    )
    for copy in y_copies:
        copy.wait_recv()
    ey = ey_all[...].reshape(n_gy * padded, rows).T
    acc[...] += dot3(split(ey), split(wy_big))

    count = n_gx * unknowns
    wide = count * planes
    sel = ones_where(over(iota((count, wide), 1), planes) == iota((count, wide), 0))
    wx = fdot(fdot_t(pick, bx[...]), fdot(mx[...], sel))
    wx_h, wx_l = split(
        jnp.where(
            over(iota((rows, wide), 0), rows_x) == rest(iota((rows, wide), 1), planes), wx, F32(0)
        )
    )
    for copy in x_copies:
        copy.wait_recv()
    ex_h, ex_l = split(ex_all[...].reshape(wide, species * lanes))
    total = acc[...] + bdot(wx_l, ex_h)
    total += bdot(
        jnp.concatenate([wx_h, wx_h], axis=1), jnp.concatenate([ex_h, ex_l], axis=0)
    )
    for s in range(species):
        q[s] = q[s] - vol[...] * total[:, part(s)]

    for copy in x_copies + y_copies + [w_copy]:
        copy.wait_send()


def per_device(n_gx, n_gy, *args):
    species_partial_mass = args[0]
    species, planes, rows_x, lanes = species_partial_mass.shape
    rows = planes * rows_x
    ins = [
        species_partial_mass.reshape(species, rows, lanes),
        *(a.reshape(2, rows, lanes) for a in args[1:4]),
        *(a.reshape(rows, lanes) for a in args[4:6]),
        *args[6:8],
        args[8].T,
        *args[9:12],
        args[12].T,
        args[13],
        *(a.reshape(1, -1) for a in args[14:17]),
        args[17].T,
        args[18].T,
        *(a.reshape(1, -1) for a in args[19:23]),
        args[23].reshape(rows, lanes),
    ]
    slots = ins[-2].shape[1]
    unknowns = args[7].shape[0]
    padded = -(-species * unknowns // 16) * 16
    wide = species * lanes
    q, fluid = pl.pallas_call(
        functools.partial(kernel, n_gx, n_gy, rows_x),
        out_shape=(
            jax.ShapeDtypeStruct((species, rows, lanes), F32),
            jax.ShapeDtypeStruct((rows, lanes), F32),
        ),
        in_specs=[pl.BlockSpec(memory_space=pl.ANY)] * INS,
        out_specs=[pl.BlockSpec(memory_space=pltpu.VMEM)] * 2,
        scratch_shapes=[
            pltpu.VMEM((n_gx, unknowns * planes, wide), F32),
            pltpu.VMEM((n_gy, padded, rows), F32),
            pltpu.VMEM((slots, lanes), F32),
            pltpu.VMEM((slots, lanes), F32),
            *([pltpu.VMEM((rows, wide), B16)] * 4),
            *([pltpu.VMEM((max(rows, slots), wide), B16)] * 2),
            pltpu.VMEM((rows, wide), F32),
            pltpu.SemaphoreType.DMA((n_gx,)),
            pltpu.SemaphoreType.DMA((n_gx,)),
            pltpu.SemaphoreType.DMA((n_gy,)),
            pltpu.SemaphoreType.DMA((n_gy,)),
            pltpu.SemaphoreType.DMA,
            pltpu.SemaphoreType.DMA,
            pltpu.SemaphoreType.DMA((INS,)),
            *(pltpu.VMEM(a.shape, a.dtype) for a in ins),
        ],
        compiler_params=pltpu.CompilerParams(
            collective_id=0, has_side_effects=True, vmem_limit_bytes=56 * 2**20
        ),
    )(*ins)
    q = q.reshape(species_partial_mass.shape)
    section_rhs = fluid.reshape(planes, rows_x, lanes)[None] * q
    section_state = species_partial_mass + 0.25 * section_rhs
    return (section_rhs, section_state)


def solution(mesh):
    grid = P(None, "gz", "gx", "gy")
    cells = P("gz", "gx", "gy")
    faces = P("gx", "gy", "gz")
    in_specs = (
        *([grid] * 4),
        *([cells] * 2),
        *([P()] * 3),
        P("gx", None),
        *([P()] * 3),
        P("gy", None),
        *([P()] * 5),
        *([faces] * 4),
        cells,
    )
    return jax.shard_map(
        functools.partial(per_device, mesh.shape["gx"], mesh.shape["gy"]),
        mesh=mesh,
        in_specs=in_specs,
        out_specs=(grid, grid),
        check_vma=False,
    )
```

```python
import functools

import jax
import jax.numpy as jnp
from jax import lax
from jax.experimental import pallas as pl
from jax.experimental.pallas import tpu as pltpu
from jax.sharding import PartitionSpec as P

HI = lax.Precision.HIGHEST
F32 = jnp.float32
B16 = jnp.bfloat16
MESH = pl.DeviceIdType.MESH
INS = 24
GROUP = 8


def shift_of(n):
    assert n & (n - 1) == 0
    return n.bit_length() - 1


def over(value, n):
    return lax.shift_right_logical(value, jnp.int32(shift_of(n)))


def rest(value, n):
    return value & (n - 1)


def iota(shape, dim):
    return lax.broadcasted_iota(jnp.int32, shape, dim)


def ones_where(mask):
    return jnp.where(mask, F32(1), F32(0))


def fdot(a, b):
    return jnp.dot(a, b, precision=HI, preferred_element_type=F32)


def fdot_t(a, b):
    return lax.dot_general(
        a, b, (((1,), (1,)), ((), ())), precision=HI, preferred_element_type=F32
    )


def bdot(a, b):
    return jnp.dot(a, b, preferred_element_type=F32)


def split(value):
    high = value.astype(B16)
    return high, (value - high.astype(F32)).astype(B16)


def dot3(a, b):
    return bdot(a[0], b[0]) + bdot(a[0], b[1]) + bdot(a[1], b[0])


def dot2(a, b):
    return bdot(a, b[0]) + bdot(a, b[1])


def kernel(
    n_gx,
    n_gy,
    rows_x,
    *refs,
):
    held = refs[-INS:]
    incoming_sem = refs[-INS - 1]
    (
        q,
        fluid_out,
        ex_all,
        ey_all,
        wall_out,
        wall_in,
        fx_h,
        fx_l,
        fy_h,
        fy_l,
        u_h,
        u_l,
        acc,
        x_send,
        x_recv,
        y_send,
        y_recv,
        w_send,
        w_recv,
    ) = refs[INS : -INS - 1]
    (
        sp,
        motion,
        g_main,
        g_cross,
        vol,
        kelvin,
        dx,
        cx,
        bx,
        mx,
        dy,
        cy,
        by,
        my,
        ln_ref,
        kexp,
        energy,
        flags,
        stoich,
        supply,
        target,
        used,
        weight,
        fluid,
    ) = held
    loads = {
        id(dst): pltpu.make_async_copy(src, dst, incoming_sem.at[i])
        for i, (src, dst) in enumerate(zip(refs[:INS], held))
    }
    first = (cx, cy, sp, motion, g_main, g_cross, supply, used, weight)
    for ref in first + tuple(ref for ref in held if all(ref is not other for other in first)):
        loads[id(ref)].start()

    def arrive(*some):
        for ref in some:
            loads[id(ref)].wait()

    species, rows, lanes = sp.shape
    planes = rows // rows_x
    unknowns = cx.shape[0]
    slots = supply.shape[1]
    reactions = flags.shape[1]
    padded = ey_all.shape[1]
    me_x, me_y, me_z = lax.axis_index("gx"), lax.axis_index("gy"), lax.axis_index("gz")

    def along_x(d):
        return {"gx": lax.rem(me_x + d, n_gx)}

    def along_y(d):
        return {"gy": lax.rem(me_y + d, n_gy)}

    across = {"gz": 1 - me_z}

    barrier = pltpu.get_barrier_semaphore()
    for d in range(1, n_gx):
        pl.semaphore_signal(barrier, inc=1, device_id=along_x(d), device_id_type=MESH)
    for d in range(1, n_gy):
        pl.semaphore_signal(barrier, inc=1, device_id=along_y(d), device_id_type=MESH)
    pl.semaphore_signal(barrier, inc=1, device_id=across, device_id_type=MESH)

    def part(s):
        return slice(s * lanes, (s + 1) * lanes)

    arrive(cx, cy)
    pick = ones_where(rest(iota((rows, rows_x), 0), rows_x) == iota((rows, rows_x), 1))
    pick_t = ones_where(rest(iota((rows_x, rows), 1), rows_x) == iota((rows_x, rows), 0))
    side = unknowns * planes
    sel = ones_where(over(iota((side, unknowns), 0), planes) == iota((side, unknowns), 1))
    cx_big = jnp.where(
        rest(iota((side, rows), 0), planes) == over(iota((side, rows), 1), rows_x),
        fdot(fdot(sel, cx[...]), pick_t),
        F32(0),
    )
    cx_h, cx_l = split(cx_big)
    cx_two = jnp.concatenate([cx_h, cx_l], axis=0)
    sel = ones_where(rest(iota((lanes, unknowns), 0), unknowns) == iota((lanes, unknowns), 1))
    cy_t = fdot(sel, cy[...]).T
    owner = over(iota((lanes, lanes), 1), unknowns)
    cy_h, cy_l = split(
        jnp.concatenate([jnp.where(owner == s, cy_t, F32(0)) for s in range(species)], axis=0)
    )

    arrive(sp, motion, g_main, g_cross)
    contra_x = g_main[0] * motion[0] + g_cross[0] * motion[1]
    for s in range(species):
        fx_h[:, part(s)], fx_l[:, part(s)] = split(contra_x * sp[s])
    both = bdot(cx_two, fx_h[...])
    ex_all[me_x] = both[:side] + both[side:] + bdot(cx_h, fx_l[...])
    pl.semaphore_wait(barrier, n_gx + n_gy - 1)
    x_copies = []
    for d in range(1, n_gx):
        copy = pltpu.make_async_remote_copy(
            src_ref=ex_all.at[me_x],
            dst_ref=ex_all.at[me_x],
            send_sem=x_send.at[d],
            recv_sem=x_recv.at[d],
            device_id=along_x(d),
            device_id_type=MESH,
        )
        copy.start()
        x_copies.append(copy)

    contra_y = g_cross[1] * motion[0] + g_main[1] * motion[1]
    for s in range(species):
        fy_h[:, part(s)], fy_l[:, part(s)] = split(contra_y * sp[s])
    both = bdot(fy_h[...], jnp.concatenate([cy_h, cy_l], axis=1))
    ey = both[:, :lanes] + both[:, lanes:] + bdot(fy_l[...], cy_h)
    ey_all[me_y] = ey.T[:padded]
    y_copies = []
    for d in range(1, n_gy):
        copy = pltpu.make_async_remote_copy(
            src_ref=ey_all.at[me_y],
            dst_ref=ey_all.at[me_y],
            send_sem=y_send.at[d],
            recv_sem=y_recv.at[d],
            device_id=along_y(d),
            device_id_type=MESH,
        )
        copy.start()
        y_copies.append(copy)

    def down(row):
        return jnp.broadcast_to(row, (lanes, slots)).T

    arrive(supply, used, weight)
    supply_col = down(supply[...])
    carried = down(weight[...] * used[...].astype(F32))
    wide = jnp.concatenate([over(supply_col, lanes)] * (rows // lanes), axis=1)
    from_rows = ones_where(wide == iota((slots, rows), 1)).astype(B16)
    from_lane = rest(supply_col, lanes) == iota((slots, lanes), 1)
    for s in range(species):
        u_h[:, part(s)], u_l[:, part(s)] = split(sp[s])
    gathered = dot2(from_rows, (u_h[...], u_l[...]))
    lane = iota((slots, lanes), 1)
    sent = jnp.zeros((slots, lanes), F32)
    for s in range(species):
        kept = jnp.where(from_lane, gathered[:, part(s)] * carried, F32(0))
        u_h[:, part(s)], u_l[:, part(s)] = split(-kept)
        sent = jnp.where(lane == s, jnp.sum(kept, axis=1, keepdims=True), sent)
    wall_out[...] = sent
    w_copy = pltpu.make_async_remote_copy(
        src_ref=wall_out,
        dst_ref=wall_in,
        send_sem=w_send,
        recv_sem=w_recv,
        device_id=across,
        device_id_type=MESH,
    )
    w_copy.start()

    arrive(kelvin, ln_ref, kexp, energy, flags, stoich)
    high, deep = reactions * GROUP, species * GROUP
    sel_r = ones_where(over(iota((high, reactions), 0), GROUP) == iota((high, reactions), 1))
    sel_s = ones_where(over(iota((species, deep), 1), GROUP) == iota((species, deep), 0))
    consumed = jnp.where(
        rest(iota((high, deep), 0), GROUP) == rest(iota((high, deep), 1), GROUP),
        fdot(fdot_t(sel_r, flags[...].astype(F32)), sel_s),
        F32(0),
    )
    sel_s = ones_where(over(iota((deep, species), 0), GROUP) == iota((deep, species), 1))
    sel_r_t = ones_where(over(iota((reactions, high), 1), GROUP) == iota((reactions, high), 0))
    shifts = jnp.where(
        rest(iota((deep, high), 0), GROUP) == rest(iota((deep, high), 1), GROUP),
        fdot(fdot(sel_s, stoich[...].astype(F32)), sel_r_t),
        F32(0),
    ).astype(B16)

    def pieces_of(value):
        top = value.astype(B16).astype(F32)
        return top, value - top

    def each_reaction(row):
        column = jnp.sum(sel_r * row, axis=1, keepdims=True)
        return pieces_of(
            jnp.where(
                rest(iota((high, GROUP), 0), GROUP) == iota((high, GROUP), 1), column, F32(0)
            )
        )

    k_h, k_l = each_reaction(kexp[...])
    e_h, e_l = each_reaction(-energy[...])
    a_h, a_l = each_reaction(ln_ref[...])
    exponents = jnp.concatenate(
        [consumed, consumed, k_h, k_h, k_l, e_h, e_h, e_l, a_h, a_l], axis=1
    ).astype(B16)
    groups = 8
    chunk = groups * GROUP

    def side_by_side(value):
        return jnp.concatenate(
            [value[g * GROUP : (g + 1) * GROUP] for g in range(groups)], axis=1
        )

    def chemistry(i, carry):
        at = pl.ds(pl.multiple_of(i * chunk, chunk), chunk)
        temperature = side_by_side(kelvin[at, :])
        t_h, t_l = pieces_of(jnp.log(temperature / F32(1500.0)))
        r_h, r_l = pieces_of(F32(1.0) / temperature - F32(1.0 / 1500.0))
        logs = [pieces_of(jnp.log(side_by_side(sp[s, at, :]))) for s in range(species)]
        one = jnp.ones_like(temperature)
        stacked = jnp.concatenate(
            [x[0] for x in logs]
            + [x[1] for x in logs]
            + [t_h, t_l, t_h, r_h, r_l, r_h, one, one],
            axis=0,
        ).astype(B16)
        progress = jnp.exp(bdot(exponents, stacked))
        made = F32(0.2) * dot2(shifts, split(progress))
        for s in range(species):
            row = made[s * GROUP : (s + 1) * GROUP]
            q[s, at, :] = jnp.concatenate([row[:, part(g)] for g in range(groups)], axis=0)
        return carry

    lax.fori_loop(0, rows // chunk, chemistry, 0)

    arrive(dx, dy, target, vol, bx, mx, by, my, fluid)
    fluid_out[...] = fluid[...].astype(F32)
    same = over(iota((rows, rows), 0), rows_x) == over(iota((rows, rows), 1), rows_x)
    dx_big = jnp.where(same, fdot(fdot(pick, dx[...]), pick_t), F32(0))
    acc[...] = dot3(split(dx_big), (fx_h[...], fx_l[...]))
    dy_h, dy_l = split(dy[...].T)
    dy_two = jnp.concatenate(
        [
            jnp.concatenate([dy_h, dy_h], axis=0),
            jnp.concatenate([dy_l, jnp.zeros_like(dy_l)], axis=0),
        ],
        axis=1,
    )
    for s in range(species):
        both = bdot(jnp.concatenate([fy_h[:, part(s)], fy_l[:, part(s)]], axis=1), dy_two)
        acc[:, part(s)] += both[:, :lanes] + both[:, lanes:]

    to_supply = ones_where(
        over(jnp.broadcast_to(supply[...], (rows, slots)), lanes) == iota((rows, slots), 0)
    ).astype(B16)
    to_target = ones_where(
        over(jnp.broadcast_to(target[...], (rows, slots)), lanes) == iota((rows, slots), 0)
    ).astype(B16)
    own_wall = dot2(to_supply, (u_h[...], u_l[...]))
    for s in range(species):
        q[s] += own_wall[:, part(s)]
    to_lane = rest(down(target[...]), lanes) == lane
    w_copy.wait_recv()
    incoming = wall_in[...]
    for s in range(species):
        spread = jnp.broadcast_to(incoming[:, s : s + 1], (slots, lanes))
        u_h[:, part(s)], u_l[:, part(s)] = split(jnp.where(to_lane, spread, F32(0)))
    far_wall = dot2(to_target, (u_h[...], u_l[...]))
    for s in range(species):
        q[s] += far_wall[:, part(s)]

    pieces = []
    for i in range(n_gy):
        shape = (padded, n_gy * unknowns)
        sel = ones_where(rest(iota(shape, 0), unknowns) + i * unknowns == iota(shape, 1))
        pieces.append(fdot(fdot_t(sel, my[...]), by[...]))
    base = jnp.concatenate(pieces, axis=0)
    owner = jnp.concatenate([over(iota((padded, lanes), 0), unknowns)] * n_gy, axis=0)
    wy_big = jnp.concatenate(
        [jnp.where(owner == s, base, F32(0)) for s in range(species)], axis=1
    )
    for copy in y_copies:
        copy.wait_recv()
    ey = ey_all[...].reshape(n_gy * padded, rows).T
    acc[...] += dot3(split(ey), split(wy_big))

    count = n_gx * unknowns
    wide = count * planes
    sel = ones_where(over(iota((count, wide), 1), planes) == iota((count, wide), 0))
    wx = fdot(fdot_t(pick, bx[...]), fdot(mx[...], sel))
    wx_h, wx_l = split(
        jnp.where(
            over(iota((rows, wide), 0), rows_x) == rest(iota((rows, wide), 1), planes), wx, F32(0)
        )
    )
    for copy in x_copies:
        copy.wait_recv()
    ex_h, ex_l = split(ex_all[...].reshape(wide, species * lanes))
    total = acc[...] + bdot(wx_l, ex_h)
    total += bdot(
        jnp.concatenate([wx_h, wx_h], axis=1), jnp.concatenate([ex_h, ex_l], axis=0)
    )
    for s in range(species):
        q[s] = q[s] - vol[...] * total[:, part(s)]

    for copy in x_copies + y_copies + [w_copy]:
        copy.wait_send()


def per_device(n_gx, n_gy, *args):
    species_partial_mass = args[0]
    species, planes, rows_x, lanes = species_partial_mass.shape
    rows = planes * rows_x
    ins = [
        species_partial_mass.reshape(species, rows, lanes),
        *(a.reshape(2, rows, lanes) for a in args[1:4]),
        *(a.reshape(rows, lanes) for a in args[4:6]),
        *args[6:8],
        args[8].T,
        *args[9:12],
        args[12].T,
        args[13],
        *(a.reshape(1, -1) for a in args[14:17]),
        args[17].T,
        args[18].T,
        *(a.reshape(1, -1) for a in args[19:23]),
        args[23].reshape(rows, lanes),
    ]
    slots = ins[-2].shape[1]
    unknowns = args[7].shape[0]
    padded = -(-species * unknowns // 16) * 16
    wide = species * lanes
    q, fluid = pl.pallas_call(
        functools.partial(kernel, n_gx, n_gy, rows_x),
        out_shape=(
            jax.ShapeDtypeStruct((species, rows, lanes), F32),
            jax.ShapeDtypeStruct((rows, lanes), F32),
        ),
        in_specs=[pl.BlockSpec(memory_space=pl.ANY)] * INS,
        out_specs=[pl.BlockSpec(memory_space=pltpu.VMEM)] * 2,
        scratch_shapes=[
            pltpu.VMEM((n_gx, unknowns * planes, wide), F32),
            pltpu.VMEM((n_gy, padded, rows), F32),
            pltpu.VMEM((slots, lanes), F32),
            pltpu.VMEM((slots, lanes), F32),
            *([pltpu.VMEM((rows, wide), B16)] * 4),
            *([pltpu.VMEM((max(rows, slots), wide), B16)] * 2),
            pltpu.VMEM((rows, wide), F32),
            pltpu.SemaphoreType.DMA((n_gx,)),
            pltpu.SemaphoreType.DMA((n_gx,)),
            pltpu.SemaphoreType.DMA((n_gy,)),
            pltpu.SemaphoreType.DMA((n_gy,)),
            pltpu.SemaphoreType.DMA,
            pltpu.SemaphoreType.DMA,
            pltpu.SemaphoreType.DMA((INS,)),
            *(pltpu.VMEM(a.shape, a.dtype) for a in ins),
        ],
        compiler_params=pltpu.CompilerParams(
            collective_id=0, has_side_effects=True, vmem_limit_bytes=56 * 2**20
        ),
    )(*ins)
    q = q.reshape(species_partial_mass.shape)
    section_rhs = fluid.reshape(planes, rows_x, lanes)[None] * q
    section_state = species_partial_mass + 0.25 * section_rhs
    return (section_rhs, section_state)


def solution(mesh):
    grid = P(None, "gz", "gx", "gy")
    cells = P("gz", "gx", "gy")
    faces = P("gx", "gy", "gz")
    in_specs = (
        *([grid] * 4),
        *([cells] * 2),
        *([P()] * 3),
        P("gx", None),
        *([P()] * 3),
        P("gy", None),
        *([P()] * 5),
        *([faces] * 4),
        cells,
    )
    return jax.shard_map(
        functools.partial(per_device, mesh.shape["gx"], mesh.shape["gy"]),
        mesh=mesh,
        in_specs=in_specs,
        out_specs=(grid, grid),
        check_vma=False,
    )
```

```python
import functools

import jax
import jax.numpy as jnp
from jax import lax
from jax.experimental import pallas as pl
from jax.experimental.pallas import tpu as pltpu
from jax.sharding import PartitionSpec as P

HI = lax.Precision.HIGHEST
F32 = jnp.float32
B16 = jnp.bfloat16
MESH = pl.DeviceIdType.MESH
INS = 24
GROUP = 8


def shift_of(n):
    assert n & (n - 1) == 0
    return n.bit_length() - 1


def over(value, n):
    return lax.shift_right_logical(value, jnp.int32(shift_of(n)))


def rest(value, n):
    return value & (n - 1)


def iota(shape, dim):
    return lax.broadcasted_iota(jnp.int32, shape, dim)


def ones_where(mask):
    return jnp.where(mask, F32(1), F32(0))


def fdot(a, b):
    return jnp.dot(a, b, precision=HI, preferred_element_type=F32)


def fdot_t(a, b):
    return lax.dot_general(
        a, b, (((1,), (1,)), ((), ())), precision=HI, preferred_element_type=F32
    )


def bdot(a, b):
    return jnp.dot(a, b, preferred_element_type=F32)


def split(value):
    high = value.astype(B16)
    return high, (value - high.astype(F32)).astype(B16)


def dot3(a, b):
    return bdot(a[0], b[0]) + bdot(a[0], b[1]) + bdot(a[1], b[0])


def dot2(a, b):
    return bdot(a, b[0]) + bdot(a, b[1])


def kernel(
    n_gx,
    n_gy,
    rows_x,
    *refs,
):
    held = refs[-INS:]
    incoming_sem = refs[-INS - 1]
    (
        q,
        fluid_out,
        ex_all,
        ey_all,
        wall_out,
        wall_in,
        fx_h,
        fx_l,
        fy_h,
        fy_l,
        u_h,
        u_l,
        acc,
        x_send,
        x_recv,
        y_send,
        y_recv,
        w_send,
        w_recv,
    ) = refs[INS : -INS - 1]
    (
        sp,
        motion,
        g_main,
        g_cross,
        vol,
        kelvin,
        dx,
        cx,
        bx,
        mx,
        dy,
        cy,
        by,
        my,
        ln_ref,
        kexp,
        energy,
        flags,
        stoich,
        supply,
        target,
        used,
        weight,
        fluid,
    ) = held
    loads = {
        id(dst): pltpu.make_async_copy(src, dst, incoming_sem.at[i])
        for i, (src, dst) in enumerate(zip(refs[:INS], held))
    }
    first = (cx, cy, sp, motion, g_main, g_cross, supply, used, weight)
    for ref in first + tuple(ref for ref in held if all(ref is not other for other in first)):
        loads[id(ref)].start()

    def arrive(*some):
        for ref in some:
            loads[id(ref)].wait()

    species, rows, lanes = sp.shape
    planes = rows // rows_x
    unknowns = cx.shape[0]
    slots = supply.shape[1]
    reactions = flags.shape[1]
    padded = ey_all.shape[1]
    me_x, me_y, me_z = lax.axis_index("gx"), lax.axis_index("gy"), lax.axis_index("gz")

    def along_x(d):
        return {"gx": lax.rem(me_x + d, n_gx)}

    def along_y(d):
        return {"gy": lax.rem(me_y + d, n_gy)}

    across = {"gz": 1 - me_z}

    barrier = pltpu.get_barrier_semaphore()
    for d in range(1, n_gx):
        pl.semaphore_signal(barrier, inc=1, device_id=along_x(d), device_id_type=MESH)
    for d in range(1, n_gy):
        pl.semaphore_signal(barrier, inc=1, device_id=along_y(d), device_id_type=MESH)
    pl.semaphore_signal(barrier, inc=1, device_id=across, device_id_type=MESH)

    def part(s):
        return slice(s * lanes, (s + 1) * lanes)

    arrive(cx, cy)
    pick = ones_where(rest(iota((rows, rows_x), 0), rows_x) == iota((rows, rows_x), 1))
    pick_t = ones_where(rest(iota((rows_x, rows), 1), rows_x) == iota((rows_x, rows), 0))
    side = unknowns * planes
    sel = ones_where(over(iota((side, unknowns), 0), planes) == iota((side, unknowns), 1))
    cx_big = jnp.where(
        rest(iota((side, rows), 0), planes) == over(iota((side, rows), 1), rows_x),
        fdot(fdot(sel, cx[...]), pick_t),
        F32(0),
    )
    cx_h, cx_l = split(cx_big)
    cx_two = jnp.concatenate([cx_h, cx_l], axis=0)
    sel = ones_where(rest(iota((lanes, unknowns), 0), unknowns) == iota((lanes, unknowns), 1))
    cy_t = fdot(sel, cy[...]).T
    owner = over(iota((lanes, lanes), 1), unknowns)
    cy_h, cy_l = split(
        jnp.concatenate([jnp.where(owner == s, cy_t, F32(0)) for s in range(species)], axis=0)
    )

    arrive(sp, motion, g_main, g_cross)
    contra_x = g_main[0] * motion[0] + g_cross[0] * motion[1]
    for s in range(species):
        fx_h[:, part(s)], fx_l[:, part(s)] = split(contra_x * sp[s])
    both = bdot(cx_two, fx_h[...])
    ex_all[me_x] = both[:side] + both[side:] + bdot(cx_h, fx_l[...])
    pl.semaphore_wait(barrier, n_gx + n_gy - 1)
    x_copies = []
    for d in range(1, n_gx):
        copy = pltpu.make_async_remote_copy(
            src_ref=ex_all.at[me_x],
            dst_ref=ex_all.at[me_x],
            send_sem=x_send.at[d],
            recv_sem=x_recv.at[d],
            device_id=along_x(d),
            device_id_type=MESH,
        )
        copy.start()
        x_copies.append(copy)

    contra_y = g_cross[1] * motion[0] + g_main[1] * motion[1]
    for s in range(species):
        fy_h[:, part(s)], fy_l[:, part(s)] = split(contra_y * sp[s])
    both = bdot(fy_h[...], jnp.concatenate([cy_h, cy_l], axis=1))
    ey = both[:, :lanes] + both[:, lanes:] + bdot(fy_l[...], cy_h)
    ey_all[me_y] = ey.T[:padded]
    y_copies = []
    for d in range(1, n_gy):
        copy = pltpu.make_async_remote_copy(
            src_ref=ey_all.at[me_y],
            dst_ref=ey_all.at[me_y],
            send_sem=y_send.at[d],
            recv_sem=y_recv.at[d],
            device_id=along_y(d),
            device_id_type=MESH,
        )
        copy.start()
        y_copies.append(copy)

    def down(row):
        return jnp.broadcast_to(row, (lanes, slots)).T

    arrive(supply, used, weight)
    supply_col = down(supply[...])
    carried = down(weight[...] * used[...].astype(F32))
    wide = jnp.concatenate([over(supply_col, lanes)] * (rows // lanes), axis=1)
    from_rows = ones_where(wide == iota((slots, rows), 1)).astype(B16)
    from_lane = rest(supply_col, lanes) == iota((slots, lanes), 1)
    for s in range(species):
        u_h[:, part(s)], u_l[:, part(s)] = split(sp[s])
    gathered = dot2(from_rows, (u_h[...], u_l[...]))
    lane = iota((slots, lanes), 1)
    sent = jnp.zeros((slots, lanes), F32)
    for s in range(species):
        kept = jnp.where(from_lane, gathered[:, part(s)] * carried, F32(0))
        u_h[:, part(s)], u_l[:, part(s)] = split(-kept)
        sent = jnp.where(lane == s, jnp.sum(kept, axis=1, keepdims=True), sent)
    wall_out[...] = sent
    w_copy = pltpu.make_async_remote_copy(
        src_ref=wall_out,
        dst_ref=wall_in,
        send_sem=w_send,
        recv_sem=w_recv,
        device_id=across,
        device_id_type=MESH,
    )
    w_copy.start()

    arrive(kelvin, ln_ref, kexp, energy, flags, stoich)
    high, deep = reactions * GROUP, species * GROUP
    sel_r = ones_where(over(iota((high, reactions), 0), GROUP) == iota((high, reactions), 1))
    sel_s = ones_where(over(iota((species, deep), 1), GROUP) == iota((species, deep), 0))
    consumed = jnp.where(
        rest(iota((high, deep), 0), GROUP) == rest(iota((high, deep), 1), GROUP),
        fdot(fdot_t(sel_r, flags[...].astype(F32)), sel_s),
        F32(0),
    )
    sel_s = ones_where(over(iota((deep, species), 0), GROUP) == iota((deep, species), 1))
    sel_r_t = ones_where(over(iota((reactions, high), 1), GROUP) == iota((reactions, high), 0))
    shifts = jnp.where(
        rest(iota((deep, high), 0), GROUP) == rest(iota((deep, high), 1), GROUP),
        fdot(fdot(sel_s, stoich[...].astype(F32)), sel_r_t),
        F32(0),
    ).astype(B16)

    def pieces_of(value):
        top = value.astype(B16).astype(F32)
        return top, value - top

    def each_reaction(row):
        column = jnp.sum(sel_r * row, axis=1, keepdims=True)
        return pieces_of(
            jnp.where(
                rest(iota((high, GROUP), 0), GROUP) == iota((high, GROUP), 1), column, F32(0)
            )
        )

    k_h, k_l = each_reaction(kexp[...])
    e_h, e_l = each_reaction(-energy[...])
    a_h, a_l = each_reaction(ln_ref[...])
    exponents = jnp.concatenate(
        [consumed, consumed, k_h, k_h, k_l, e_h, e_h, e_l, a_h, a_l], axis=1
    ).astype(B16)
    groups = 16
    chunk = groups * GROUP

    def side_by_side(value):
        return jnp.concatenate(
            [value[g * GROUP : (g + 1) * GROUP] for g in range(groups)], axis=1
        )

    def chemistry(i, carry):
        at = pl.ds(pl.multiple_of(i * chunk, chunk), chunk)
        temperature = side_by_side(kelvin[at, :])
        t_h, t_l = pieces_of(jnp.log(temperature / F32(1500.0)))
        r_h, r_l = pieces_of(F32(1.0) / temperature - F32(1.0 / 1500.0))
        logs = [pieces_of(jnp.log(side_by_side(sp[s, at, :]))) for s in range(species)]
        one = jnp.ones_like(temperature)
        stacked = jnp.concatenate(
            [x[0] for x in logs]
            + [x[1] for x in logs]
            + [t_h, t_l, t_h, r_h, r_l, r_h, one, one],
            axis=0,
        ).astype(B16)
        progress = jnp.exp(bdot(exponents, stacked))
        made = F32(0.2) * dot2(shifts, split(progress))
        for s in range(species):
            row = made[s * GROUP : (s + 1) * GROUP]
            q[s, at, :] = jnp.concatenate([row[:, part(g)] for g in range(groups)], axis=0)
        return carry

    lax.fori_loop(0, rows // chunk, chemistry, 0)

    arrive(dx, dy, target, vol, bx, mx, by, my, fluid)
    fluid_out[...] = fluid[...].astype(F32)
    same = over(iota((rows, rows), 0), rows_x) == over(iota((rows, rows), 1), rows_x)
    dx_big = jnp.where(same, fdot(fdot(pick, dx[...]), pick_t), F32(0))
    acc[...] = dot3(split(dx_big), (fx_h[...], fx_l[...]))
    dy_h, dy_l = split(dy[...].T)
    dy_two = jnp.concatenate(
        [
            jnp.concatenate([dy_h, dy_h], axis=0),
            jnp.concatenate([dy_l, jnp.zeros_like(dy_l)], axis=0),
        ],
        axis=1,
    )
    for s in range(species):
        both = bdot(jnp.concatenate([fy_h[:, part(s)], fy_l[:, part(s)]], axis=1), dy_two)
        acc[:, part(s)] += both[:, :lanes] + both[:, lanes:]

    to_supply = ones_where(
        over(jnp.broadcast_to(supply[...], (rows, slots)), lanes) == iota((rows, slots), 0)
    ).astype(B16)
    to_target = ones_where(
        over(jnp.broadcast_to(target[...], (rows, slots)), lanes) == iota((rows, slots), 0)
    ).astype(B16)
    own_wall = dot2(to_supply, (u_h[...], u_l[...]))
    for s in range(species):
        q[s] += own_wall[:, part(s)]
    to_lane = rest(down(target[...]), lanes) == lane
    w_copy.wait_recv()
    incoming = wall_in[...]
    for s in range(species):
        spread = jnp.broadcast_to(incoming[:, s : s + 1], (slots, lanes))
        u_h[:, part(s)], u_l[:, part(s)] = split(jnp.where(to_lane, spread, F32(0)))
    far_wall = dot2(to_target, (u_h[...], u_l[...]))
    for s in range(species):
        q[s] += far_wall[:, part(s)]

    pieces = []
    for i in range(n_gy):
        shape = (padded, n_gy * unknowns)
        sel = ones_where(rest(iota(shape, 0), unknowns) + i * unknowns == iota(shape, 1))
        pieces.append(fdot(fdot_t(sel, my[...]), by[...]))
    base = jnp.concatenate(pieces, axis=0)
    owner = jnp.concatenate([over(iota((padded, lanes), 0), unknowns)] * n_gy, axis=0)
    wy_big = jnp.concatenate(
        [jnp.where(owner == s, base, F32(0)) for s in range(species)], axis=1
    )
    for copy in y_copies:
        copy.wait_recv()
    ey = ey_all[...].reshape(n_gy * padded, rows).T
    acc[...] += dot3(split(ey), split(wy_big))

    count = n_gx * unknowns
    wide = count * planes
    sel = ones_where(over(iota((count, wide), 1), planes) == iota((count, wide), 0))
    wx = fdot(fdot_t(pick, bx[...]), fdot(mx[...], sel))
    wx_h, wx_l = split(
        jnp.where(
            over(iota((rows, wide), 0), rows_x) == rest(iota((rows, wide), 1), planes), wx, F32(0)
        )
    )
    for copy in x_copies:
        copy.wait_recv()
    ex_h, ex_l = split(ex_all[...].reshape(wide, species * lanes))
    total = acc[...] + bdot(wx_l, ex_h)
    total += bdot(
        jnp.concatenate([wx_h, wx_h], axis=1), jnp.concatenate([ex_h, ex_l], axis=0)
    )
    for s in range(species):
        q[s] = q[s] - vol[...] * total[:, part(s)]

    for copy in x_copies + y_copies + [w_copy]:
        copy.wait_send()


def per_device(n_gx, n_gy, *args):
    species_partial_mass = args[0]
    species, planes, rows_x, lanes = species_partial_mass.shape
    rows = planes * rows_x
    ins = [
        species_partial_mass.reshape(species, rows, lanes),
        *(a.reshape(2, rows, lanes) for a in args[1:4]),
        *(a.reshape(rows, lanes) for a in args[4:6]),
        *args[6:8],
        args[8].T,
        *args[9:12],
        args[12].T,
        args[13],
        *(a.reshape(1, -1) for a in args[14:17]),
        args[17].T,
        args[18].T,
        *(a.reshape(1, -1) for a in args[19:23]),
        args[23].reshape(rows, lanes),
    ]
    slots = ins[-2].shape[1]
    unknowns = args[7].shape[0]
    padded = -(-species * unknowns // 16) * 16
    wide = species * lanes
    q, fluid = pl.pallas_call(
        functools.partial(kernel, n_gx, n_gy, rows_x),
        out_shape=(
            jax.ShapeDtypeStruct((species, rows, lanes), F32),
            jax.ShapeDtypeStruct((rows, lanes), F32),
        ),
        in_specs=[pl.BlockSpec(memory_space=pl.ANY)] * INS,
        out_specs=[pl.BlockSpec(memory_space=pltpu.VMEM)] * 2,
        scratch_shapes=[
            pltpu.VMEM((n_gx, unknowns * planes, wide), F32),
            pltpu.VMEM((n_gy, padded, rows), F32),
            pltpu.VMEM((slots, lanes), F32),
            pltpu.VMEM((slots, lanes), F32),
            *([pltpu.VMEM((rows, wide), B16)] * 4),
            *([pltpu.VMEM((max(rows, slots), wide), B16)] * 2),
            pltpu.VMEM((rows, wide), F32),
            pltpu.SemaphoreType.DMA((n_gx,)),
            pltpu.SemaphoreType.DMA((n_gx,)),
            pltpu.SemaphoreType.DMA((n_gy,)),
            pltpu.SemaphoreType.DMA((n_gy,)),
            pltpu.SemaphoreType.DMA,
            pltpu.SemaphoreType.DMA,
            pltpu.SemaphoreType.DMA((INS,)),
            *(pltpu.VMEM(a.shape, a.dtype) for a in ins),
        ],
        compiler_params=pltpu.CompilerParams(
            collective_id=0, has_side_effects=True, vmem_limit_bytes=56 * 2**20
        ),
    )(*ins)
    q = q.reshape(species_partial_mass.shape)
    section_rhs = fluid.reshape(planes, rows_x, lanes)[None] * q
    section_state = species_partial_mass + 0.25 * section_rhs
    return (section_rhs, section_state)


def solution(mesh):
    grid = P(None, "gz", "gx", "gy")
    cells = P("gz", "gx", "gy")
    faces = P("gx", "gy", "gz")
    in_specs = (
        *([grid] * 4),
        *([cells] * 2),
        *([P()] * 3),
        P("gx", None),
        *([P()] * 3),
        P("gy", None),
        *([P()] * 5),
        *([faces] * 4),
        cells,
    )
    return jax.shard_map(
        functools.partial(per_device, mesh.shape["gx"], mesh.shape["gy"]),
        mesh=mesh,
        in_specs=in_specs,
        out_specs=(grid, grid),
        check_vma=False,
    )
```
